512 devices in a mesh: dp: 8 (over x, core), ctx: 64 (over z, y).
Axes of the slice: x: 4, y: 8, z: 8, core: 2. Of those that a mesh axis runs over, the one named last changes fastest.
Arguments:
- query: bfloat16 [32768, 2048], P('ctx', 'dp'), may hold values from -6 to 6
- key_in: bfloat16 [32768, 2048], P('ctx', 'dp'), may hold values from -6 to 6
- value: bfloat16 [32768, 2048], P('ctx', 'dp'), may hold values from -6 to 6
- latent: bfloat16 [32768, 16], P('ctx'), may hold values from -24 to 24
- w_b: bfloat16 [16, 2048], P(None, 'dp'), may hold values from -1.5 to 1.5
- gate_bias: float32 [2048], P('dp'), may hold values from -1 to 10
- doc_ids: int32 [32768], P('ctx'), may hold values from 0 to 31, as said below
- d_out: bfloat16 [32768, 2048], P('ctx', 'dp'), may hold values from -6 to 6
Outputs:
- output: bfloat16 [32768, 2048], P('ctx', 'dp')
- grad_query: bfloat16 [32768, 2048], P('ctx', 'dp')
- sensitivity_addresses: bfloat16 [32768, 2048], P('ctx', 'dp')
- grad_value: bfloat16 [32768, 2048], P('ctx', 'dp')
- grad_latent: float32 [32768, 16], P('ctx')
- grad_w_b: float32 [16, 2048], P(None, 'dp')
- grad_gate_bias: float32 [2048], P('dp')
The draws below stay inside these ranges and needn't reach their ends.
Inputs may be any that keep to these rules, and one draw needn't show every extreme that they name: doc_ids never fall and number 32 documents; a document holds 1 to 3072 positions; the first holds exactly 3072.
All inputs are finite; a program needn't handle non-finite values.
Results may differ from the reference program's by a relative error of at most 0.0013.
Values sent between devices are 32-bit elements; how exact they have to be, the bound alone decides.
No kernel may reach another device: no remote copies, remote signals or barrier semaphores. Data moves between devices by JAX's collectives and lax.ppermute only.
A program may use at most 64 MiB of HBM per device.

```python
import jax
import jax.numpy as jnp
from jax import lax

HEADS = 16
HEAD = 128
RANK = 16
GROUP = 64
STRAND_SPAN = 32768
HD = 2048
MOST = 3072
DOCS = 32


def draw_latent(key, part):
    key = jax.random.fold_in(key, 11)
    primary_seed_handle, spike_seed_handle = jax.random.split(key, 2)
    starting_figure = jnp.clip(jax.random.normal(primary_seed_handle, (STRAND_SPAN, RANK), jnp.float32), -4.0, 4.0)
    spike_sample = jax.random.bernoulli(spike_seed_handle, 1.0 / 64.0, (STRAND_SPAN, 1))
    return (starting_figure * jnp.where(spike_sample, 6.0, 1.0)).astype(jnp.bfloat16)


def draw_gate_bias(key, part):
    key = jax.random.fold_in(key, 23)
    return jax.random.uniform(key, (HD,), jnp.float32, -1.0, 10.0)


def draw_doc_ids(key, part):
    key = jax.random.fold_in(key, 37)
    stride = (STRAND_SPAN - MOST) // (DOCS - 1)
    jitter = jax.random.randint(key, (DOCS - 1,), 0, max(stride // 2, 1), jnp.int32)
    order = jnp.arange(DOCS - 1, dtype=jnp.int32)
    jitter = jnp.where(order == 0, 0, jitter)
    starts = MOST + order * stride + jitter
    positions = jnp.arange(STRAND_SPAN, dtype=jnp.int32)
    return jnp.sum((positions[:, None] >= starts[None, :]).astype(jnp.int32), axis=1).astype(jnp.int32)


def block_scale(stream_key, dims, shards, least, largest):
    loudness = 1.0
    for dim, parts in shards:
        draws = jax.random.uniform(jax.random.fold_in(jax.random.fold_in(stream_key, 6), dim), (parts,), jnp.float32, least / len(shards), largest / len(shards))
        loudness = loudness * jnp.repeat(jnp.exp(draws), dims[dim] // parts).reshape((-1,) + (1,) * (len(dims) - 1 - dim))
    return loudness


def normal_values(stream_key, shape, scale, most, cuts=(), kind=jnp.bfloat16):
    array = scale * jax.random.normal(stream_key, shape, jnp.float32)
    if cuts:
        array = array * block_scale(stream_key, shape, cuts, -0.22, 0.18)
    return jnp.clip(array, -most, most).astype(kind)


def setup_inputs(seed: int = 0) -> dict:
    streams_of = jax.random.split(jax.random.key(seed), 9)
    return {
        "query": normal_values(streams_of[0], (STRAND_SPAN, HD), 1.0, 6.0, ((0, 64), (1, 8))),
        "key_in": normal_values(streams_of[1], (STRAND_SPAN, HD), 1.0, 6.0, ((0, 64), (1, 8))),
        "value": normal_values(streams_of[2], (STRAND_SPAN, HD), 1.0, 6.0, ((0, 64), (1, 8))),
        "latent": draw_latent(jax.random.fold_in(streams_of[8], 71), 0),
        "w_b": normal_values(streams_of[4], (RANK, HD), RANK ** -0.5, 1.5, ((1, 8),)),
        "gate_bias": draw_gate_bias(jax.random.fold_in(streams_of[8], 71), 0),
        "doc_ids": draw_doc_ids(jax.random.fold_in(streams_of[8], 71), 0),
        "d_out": normal_values(streams_of[7], (STRAND_SPAN, HD), 1.0, 6.0, ((0, 64), (1, 8))),
    }


precise_mode = lax.Precision.HIGHEST

def group_pass(carried_in, pieces):
    memory_state, prev_id = carried_in
    queries, address_share, values_portion, log_gate, segment = pieces
    decay_sum = jnp.cumsum(log_gate, axis=0)
    positions = jnp.arange(segment.shape[0])
    visible = (positions[:, None] >= positions[None, :]) & (segment[:, None] == segment[None, :])
    query_decay = queries * jnp.exp(decay_sum)
    k_decay = address_share * jnp.exp(-decay_sum)
    scores = jnp.einsum('ihk,jhk->hij', query_decay, k_decay, precision=precise_mode)
    scores = jnp.where(visible[None], scores, 0.0)
    inner = jnp.einsum('hij,jhv->ihv', scores, values_portion, precision=precise_mode)
    leading_mask = (segment == prev_id).astype(jnp.float32)
    outer_product = leading_mask[:, None, None] * jnp.einsum('scd,cdx->scx', query_decay, memory_state, precision=precise_mode)
    result = (inner + outer_product) * HEAD ** (-0.5)
    last_id = segment[-1]
    total_decay = decay_sum[-1]
    tail_mask = (segment == last_id).astype(jnp.float32)
    key_tail_decay = address_share * jnp.exp(total_decay[None] - decay_sum) * tail_mask[:, None, None]
    keep_state_flag = (last_id == prev_id).astype(jnp.float32)
    memory_state = keep_state_flag * jnp.exp(total_decay)[:, :, None] * memory_state + jnp.einsum('upw,upl->pwl', key_tail_decay, values_portion, precision=precise_mode)
    return ((memory_state, last_id), result)

def gate_logs(latent_part, weight_part, bias_part):
    gate_pre = jnp.dot(latent_part, weight_part, precision=precise_mode) + bias_part
    return jnp.maximum(jax.nn.log_sigmoid(gate_pre) / 16.0, -0.5)

def head_out(queries, address_share, values_portion, latent_part, weight_part, bias_part, segment):
    log_gate = gate_logs(latent_part, weight_part, bias_part)
    pieces = tuple((source.reshape(-1, GROUP, 1, HEAD) for source in (queries, address_share, values_portion, log_gate)))
    initial = (jnp.zeros((1, HEAD, HEAD), jnp.float32), jnp.int32(-1))
    _, result = lax.scan(group_pass, initial, pieces + (segment.reshape(-1, GROUP),))
    return result.reshape(STRAND_SPAN, HEAD)

def reference(query, key_in, value, latent, w_b, gate_bias, doc_ids, d_out):
    weight_full = w_b.astype(jnp.float32)
    latent_full = latent.astype(jnp.float32)

    def per_head(head_index):
        start = (head_index * HEAD).astype(jnp.int32)

        def columns(source):
            return lax.dynamic_slice_in_dim(source, start, HEAD, 1)

        def single(query_part, key_part, value_part, latent_part, weight_part, bias_part):
            return head_out(query_part, key_part, value_part, latent_part, weight_part, bias_part, doc_ids)
        operands = (columns(query).astype(jnp.float32), columns(key_in).astype(jnp.float32), columns(value).astype(jnp.float32), latent_full, columns(weight_full), lax.dynamic_slice_in_dim(gate_bias, start, HEAD, 0))
        result, pullback = jax.vjp(single, *operands)
        grads = pullback(columns(d_out).astype(jnp.float32))
        return (result,) + tuple(grads)
    stacked = lax.map(per_head, jnp.arange(HEADS, dtype=jnp.int32))
    result, grad_q, grad_k, grad_v, grad_lat, grad_w, grad_b = stacked

    def joined(source):
        return jnp.transpose(source, (1, 0, 2)).reshape(source.shape[1], HD)
    return (joined(result).astype(jnp.bfloat16), joined(grad_q).astype(jnp.bfloat16), joined(grad_k).astype(jnp.bfloat16), joined(grad_v).astype(jnp.bfloat16), lax.optimization_barrier(jnp.sum(grad_lat, axis=0)), joined(grad_w), grad_b.reshape(HD))
```

```python
import jax
import jax.numpy as jnp
from jax import lax
from jax.experimental import pallas as pl
from jax.experimental.pallas import tpu as pltpu
from jax.sharding import Mesh
from jax.sharding import PartitionSpec as P

HEAD = 128
RANK = 16
SPAN = 512
CHUNK = 128
PARTS = SPAN // CHUNK
SCALE = HEAD ** (-0.5)
RING = 8
CTX = ("z", "y")
DP = ("x", "core")

F32 = jnp.float32
BF16 = jnp.bfloat16
NN = (((1,), (0,)), ((), ()))
NT = (((1,), (1,)), ((), ()))
TN = (((0,), (0,)), ((), ()))


def split2(x):
    high = x.astype(BF16)
    return high, (x - high.astype(F32)).astype(BF16)


def split3(x):
    high = x.astype(BF16)
    rest = x - high.astype(F32)
    middle = rest.astype(BF16)
    return high, middle, (rest - middle.astype(F32)).astype(BF16)


def dot(a, b, dims):
    return lax.dot_general(a, b, dims, preferred_element_type=F32)


def dot_left(a, parts, dims):
    (ca,), (cb,) = dims[0]
    return dot(jnp.concatenate([a] * len(parts), axis=ca), jnp.concatenate(parts, axis=cb), dims)


def dot_right(parts, b, dims):
    (ca,), (cb,) = dims[0]
    return dot(jnp.concatenate(parts, axis=ca), jnp.concatenate([b] * len(parts), axis=cb), dims)


def dot_both(a, b, dims):
    (ca,), (cb,) = dims[0]
    left = jnp.concatenate([a[0], a[1], a[0]], axis=ca)
    right = jnp.concatenate([b[0], b[0], b[1]], axis=cb)
    return dot(left, right, dims)


def places():
    rows = lax.broadcasted_iota(jnp.int32, (CHUNK, CHUNK), 0)
    columns = lax.broadcasted_iota(jnp.int32, (CHUNK, CHUNK), 1)
    return rows, columns


def segments(doc_ref, c):
    rows, columns = places()
    row = doc_ref[c : c + 1, :]
    column = jnp.sum(jnp.where(rows == columns, row, 0.0), axis=1, keepdims=True)
    return row, column, row[:, :1], row[:, CHUNK - 1 :]


def as_number(flag):
    return flag.astype(F32)


def state_kernel(
    lat_ref, w_ref, bias_ref, doc_ref, q_ref, k_ref, v_ref, d_ref,
    send_ref, decay_ref, slope_ref, mem_ref, pull_ref,
):
    heads = q_ref.shape[1] // HEAD
    rows, columns = places()
    lower = (rows >= columns).astype(BF16)
    gate_pre = dot(lat_ref[...], w_ref[...], TN) + bias_ref[...]
    small = jnp.exp(-jnp.abs(gate_pre))
    series = small * (1.0 - small * (0.5 - small * (1.0 / 3.0 - small * (0.25 - small * 0.2))))
    log_one = jnp.where(small < 0.02, series, jnp.log(1.0 + small))
    log_gate = -(jnp.maximum(-gate_pre, 0.0) + log_one) / 16.0
    sigmoid = jnp.where(gate_pre >= 0.0, small, 1.0) / (1.0 + small)
    free = jnp.where(log_gate > -0.5, 1.0, jnp.where(log_gate == -0.5, 0.5, 0.0))
    slope_ref[...] = free * sigmoid * (1.0 / 16.0)
    log_gate = jnp.maximum(log_gate, -0.5)
    lower3 = jnp.concatenate([lower] * 3, axis=1)
    for c in range(PARTS):
        at = slice(c * CHUNK, (c + 1) * CHUNK)
        decay_ref[at, :] = dot(lower3, jnp.concatenate(split3(log_gate[at, :]), axis=0), NN)

    seg = [segments(doc_ref, c) for c in range(PARTS)]
    factors = []
    for h in range(heads):
        on = slice(h * HEAD, (h + 1) * HEAD)
        total = None
        memory = None
        pulls, keeps = [], []
        for c in range(PARTS):
            at = slice(c * CHUNK, (c + 1) * CHUNK)
            _, column, first, last = seg[c]
            decay = decay_ref[at, on]
            end = decay[CHUNK - 1 :, :]
            key_tail = k_ref[at, on].astype(F32) * jnp.exp(end - decay) * as_number(column == last)
            added = dot_left(v_ref[at, on], split2(key_tail), TN)
            query_lead = (
                q_ref[at, on].astype(F32) * jnp.exp(decay) * (as_number(column == first) * SCALE)
            )
            pulled = dot_left(d_ref[at, on], split2(query_lead), TN)
            mem_ref[h, c] = added
            pull_ref[h, c] = pulled
            keep = jnp.exp(end) * as_number(first == last)
            keeps.append(keep)
            pulls.append(pulled)
            if c == 0:
                memory, total = added, end
            else:
                memory = added + keep * as_number(first == seg[c - 1][3]) * memory
                total = total + end
        back = pulls[-1]
        for c in reversed(range(PARTS - 1)):
            back = pulls[c] + keeps[c] * as_number(seg[c][3] == seg[c + 1][2]) * back
        whole = jnp.exp(total) * as_number(seg[0][2] == seg[-1][3])
        factors.append(whole)
        each = HEAD // RING
        for j in range(RING):
            send_ref[j, h * each : (h + 1) * each, :] = memory[j * each : (j + 1) * each, :]
            start = heads * each + h * each
            send_ref[j, start : start + each, :] = back[j * each : (j + 1) * each, :]
    ids = [jnp.broadcast_to(seg[0][2] + 1.0, (1, HEAD)), jnp.broadcast_to(seg[-1][3] + 1.0, (1, HEAD))]
    small_rows = jnp.concatenate(factors + ids + [jnp.zeros((4, HEAD), F32)], axis=0)
    for j in range(RING):
        send_ref[j, 64:, :] = small_rows


def taken(got_ref, j):
    factor = jnp.concatenate(
        [jnp.broadcast_to(got_ref[j, 64 + h : 65 + h, :], (16, HEAD)) for h in range(2)], axis=0
    )
    return got_ref[j, 0:32, :], got_ref[j, 32:64, :], factor, got_ref[j, 66:67, :], got_ref[j, 67:68, :]


def total_kernel(got_ref, ahead_ref, behind_ref):
    got = [taken(got_ref, j) for j in range(RING)]
    memory = got[0][0]
    for j in range(1, RING):
        memory = got[j][0] + got[j][2] * as_number(got[j][3] == got[j - 1][4]) * memory
    back = got[-1][1]
    for j in reversed(range(RING - 1)):
        back = got[j][1] + got[j][2] * as_number(got[j][4] == got[j + 1][3]) * back
    zeros = jnp.zeros((7, HEAD), F32)
    ahead_ref[...] = jnp.concatenate([memory, got[-1][4], zeros], axis=0)
    behind_ref[...] = jnp.concatenate([back, got[0][3], zeros], axis=0)


def spread_kernel(got_ref, ahead_ref, behind_ref, send_ref):
    got = [taken(got_ref, j) for j in range(RING)]
    memory = as_number(got[0][3] == ahead_ref[32:33, :]) * ahead_ref[0:32, :]
    for j in range(RING):
        send_ref[j, 0:32, :] = memory
        if j < RING - 1:
            memory = as_number(got[j][4] == got[j + 1][3]) * (got[j][0] + got[j][2] * memory)
    back = as_number(got[-1][4] == behind_ref[32:33, :]) * behind_ref[0:32, :]
    for j in reversed(range(RING)):
        send_ref[j, 32:64, :] = back
        if j > 0:
            back = as_number(got[j - 1][4] == got[j][3]) * (got[j][1] + got[j][2] * back)


def main_kernel(
    lat_ref, w_ref, doc_ref, q_ref, k_ref, v_ref, d_ref, decay_ref, slope_ref, mem_ref, pull_ref,
    got_ref, out_ref, dq_ref, dk_ref, dv_ref, lat_send_ref, w_send_ref,
):
    heads = q_ref.shape[1] // HEAD
    rows, columns = places()
    seg = [segments(doc_ref, c) for c in range(PARTS)]
    earlier = rows >= columns
    masks = [earlier & (seg[c][1] == seg[c][0]) for c in range(PARTS)]
    later = [((columns >= rows) & (seg[c][1] == seg[c][0])).astype(BF16) for c in range(PARTS)]
    grad_lat = None
    grad_w = [None] * heads
    grad_b = [None] * heads
    grad_pre_parts = [[None] * heads for _ in range(PARTS)]
    for h in range(heads):
        on = slice(h * HEAD, (h + 1) * HEAD)
        memory = got_ref[:, h * 16 : (h + 1) * 16, :].reshape(HEAD, HEAD)
        back = got_ref[:, 32 + h * 16 : 48 + h * 16, :].reshape(HEAD, HEAD)
        starts, ends, backs = [], [], [None] * PARTS
        keeps = []
        for c in range(PARTS):
            _, _, first, last = seg[c]
            end = decay_ref[(c + 1) * CHUNK - 1 : (c + 1) * CHUNK, on]
            keeps.append(jnp.exp(end) * as_number(first == last))
            if c > 0:
                memory = memory * as_number(first == seg[c - 1][3])
            starts.append(memory)
            memory = mem_ref[h, c] + keeps[c] * memory
            ends.append(memory)
        for c in reversed(range(PARTS)):
            backs[c] = back
            if c > 0:
                back = as_number(seg[c][2] == seg[c - 1][3]) * (pull_ref[h, c] + keeps[c] * back)
        for c in range(PARTS):
            at = slice(c * CHUNK, (c + 1) * CHUNK)
            _, column, first, last = seg[c]
            lead, tail = as_number(column == first), as_number(column == last)
            q, k, v, d = q_ref[at, on], k_ref[at, on], v_ref[at, on], d_ref[at, on]
            q32, k32 = q.astype(F32), k.astype(F32)
            decay = decay_ref[at, on]
            end = decay[CHUNK - 1 :, :]
            grow = jnp.exp(decay)
            shrink = jnp.exp(-decay)
            rest = jnp.exp(end - decay) * tail
            qd = split2(q32 * grow)
            kd = split2(k32 * shrink)
            kt = split2(k32 * rest)
            start, behind = split2(starts[c]), split2(backs[c])
            scores = split2(jnp.where(masks[c], dot_both(qd, kd, NT), 0.0))
            pulls = split2(jnp.where(masks[c], dot(d, v, NT), 0.0))
            out = dot_right(scores, v, NN) + lead * dot_both(qd, start, NT)
            out_ref[at, on] = (out * SCALE).astype(BF16)
            dq = (dot_both(pulls, kd, NN) + lead * dot_left(d, start, NN)) * (grow * SCALE)
            dk = dot_both(pulls, qd, TN) * (shrink * SCALE) + rest * dot_left(v, behind, NN)
            dv = dot_right(scores, d, TN) * SCALE + dot_both(kt, behind, NT)
            dq_ref[at, on] = dq.astype(BF16)
            dk_ref[at, on] = dk.astype(BF16)
            dv_ref[at, on] = dv.astype(BF16)
            through = jnp.sum(ends[c] * backs[c], axis=0, keepdims=True)
            grad_gate = dot_left(later[c], split3(q32 * dq - k32 * dk), NN) + tail * through
            grad_pre = grad_gate * slope_ref[at, on]
            grad_b[h] = jnp.sum(grad_pre, axis=0, keepdims=True) + (0.0 if c == 0 else grad_b[h])
            grad_pre_parts[c][h] = split2(grad_pre)
    w = w_ref[...]
    lat_parts = []
    for c in range(PARTS):
        pre = tuple(
            jnp.concatenate([grad_pre_parts[c][h][i] for h in range(heads)], axis=1) for i in range(2)
        )
        lat_parts.append(dot(w, pre[0], NT) + dot(w, pre[1], NT))
        lat = lat_ref[:, c * CHUNK : (c + 1) * CHUNK]
        for h in range(heads):
            add = dot_left(lat, grad_pre_parts[c][h], NN)
            grad_w[h] = add if c == 0 else grad_w[h] + add
    zeros = jnp.zeros((7, HEAD), F32)
    lat_send = jnp.concatenate(lat_parts, axis=0)
    w_send = jnp.concatenate(
        [x for h in range(heads) for x in (grad_w[h], grad_b[h], zeros)], axis=0
    )
    for j in range(RING):
        lat_send_ref[j] = lat_send
        w_send_ref[j] = w_send


def resend_kernel(got_ref, send_ref):
    total = got_ref[0]
    for j in range(1, RING):
        total = total + got_ref[j]
    for j in range(RING):
        send_ref[j] = total


def finish_kernel(lat_got_ref, w_got_ref, lat_ref, w_ref, b_ref):
    total = lat_got_ref[0]
    for j in range(1, RING):
        total = total + lat_got_ref[j]
    for c in range(PARTS):
        lat_ref[:, c * CHUNK : (c + 1) * CHUNK] = total[c * RANK : (c + 1) * RANK, :]
    total = w_got_ref[0]
    for j in range(1, RING):
        total = total + w_got_ref[j]
    for h in range(2):
        on = slice(h * HEAD, (h + 1) * HEAD)
        w_ref[:, on] = total[h * 24 : h * 24 + RANK, :]
        b_ref[:, on] = total[h * 24 + RANK : h * 24 + RANK + 1, :]


def call(kernel, outs, *operands):
    whole = pl.BlockSpec(memory_space=pltpu.VMEM)
    return pl.pallas_call(
        kernel,
        out_shape=outs,
        in_specs=[whole] * len(operands),
        out_specs=jax.tree.map(lambda _: whole, outs),
        compiler_params=pltpu.CompilerParams(vmem_limit_bytes=40 * 2**20),
    )(*operands)


def shape(dims, kind=F32):
    return jax.ShapeDtypeStruct(dims, kind)


def exchange(x, axis):
    return lax.all_to_all(x, axis, 0, 0)


def passed(value, axis, steps):
    count = lax.axis_size(axis)
    pairs = [(s, s + steps) for s in range(count) if 0 <= s + steps < count]
    return lax.ppermute(value, axis, pairs)


def body(query, key_in, value, latent, w_b, gate_bias, doc_ids, d_out):
    tokens, width = query.shape
    heads = width // HEAD
    lat = latent.T
    bias = gate_bias.reshape(1, width)
    docs = doc_ids.astype(F32).reshape(PARTS, CHUNK)
    wide = shape((tokens, width))
    states = shape((heads, PARTS, HEAD, HEAD))
    send, decay, slope, mem, pull = call(
        state_kernel, (shape((RING, 72, HEAD)), wide, wide, states, states),
        lat, w_b, bias, docs, query, key_in, value, d_out,
    )
    got = exchange(send, "y")
    ahead, behind = call(total_kernel, (shape((40, HEAD)), shape((40, HEAD))), got)
    ahead, behind = passed(ahead, "z", 1), passed(behind, "z", -1)
    back = call(spread_kernel, shape((RING, 64, HEAD)), got, ahead, behind)
    carried = exchange(back, "y")
    half = shape((tokens, width), BF16)
    out, grad_q, grad_k, grad_v, lat_send, w_send = call(
        main_kernel,
        (half, half, half, half, shape((RING, PARTS * RANK, HEAD)), shape((RING, 48, HEAD))),
        lat, w_b, docs, query, key_in, value, d_out, decay, slope, mem, pull, carried,
    )
    w_got = exchange(w_send, "y")
    w_send = call(resend_kernel, shape((RING, 48, HEAD)), w_got)
    w_got = exchange(w_send, "z")
    lat_got = exchange(lat_send, DP)
    grad_lat, grad_w, grad_b = call(
        finish_kernel, (shape((RANK, tokens)), shape((RANK, width)), shape((1, width))), lat_got, w_got
    )
    return out, grad_q, grad_k, grad_v, grad_lat.T, grad_w, grad_b.reshape(width)


def solution(mesh):
    grid = Mesh(mesh.devices.reshape(4, 2, RING, RING), ("x", "core", "z", "y"))
    rows = P(CTX, DP)
    in_specs = (rows, rows, rows, P(CTX, None), P(None, DP), P(DP), P(CTX), rows)
    out_specs = (rows, rows, rows, rows, P(CTX, None), P(None, DP), P(DP))
    return jax.shard_map(body, mesh=grid, in_specs=in_specs, out_specs=out_specs, check_vma=False)
```

```python
import jax
import jax.numpy as jnp
from jax import lax
from jax.experimental import pallas as pl
from jax.experimental.pallas import tpu as pltpu
from jax.sharding import Mesh
from jax.sharding import PartitionSpec as P

HEAD = 128
RANK = 16
SPAN = 512
CHUNK = 128
PARTS = SPAN // CHUNK
SCALE = HEAD ** (-0.5)
RING = 8
HELD = 16
INNER_HELD = 16
INNER_FLOPS = 4 * 10**10
CTX = ("z", "y")
DP = ("x", "core")

F32 = jnp.float32
BF16 = jnp.bfloat16
NN = (((1,), (0,)), ((), ()))
NT = (((1,), (1,)), ((), ()))
TN = (((0,), (0,)), ((), ()))


def split2(x):
    high = x.astype(BF16)
    return high, (x - high.astype(F32)).astype(BF16)


def split3(x):
    high = x.astype(BF16)
    rest = x - high.astype(F32)
    middle = rest.astype(BF16)
    return high, middle, (rest - middle.astype(F32)).astype(BF16)


def dot(a, b, dims):
    return lax.dot_general(a, b, dims, preferred_element_type=F32)


def dot_left(a, parts, dims):
    (ca,), (cb,) = dims[0]
    return dot(jnp.concatenate([a] * len(parts), axis=ca), jnp.concatenate(parts, axis=cb), dims)


def dot_right(parts, b, dims):
    (ca,), (cb,) = dims[0]
    return dot(jnp.concatenate(parts, axis=ca), jnp.concatenate([b] * len(parts), axis=cb), dims)


def dot_both(a, b, dims):
    (ca,), (cb,) = dims[0]
    left = jnp.concatenate([a[0], a[1], a[0]], axis=ca)
    right = jnp.concatenate([b[0], b[0], b[1]], axis=cb)
    return dot(left, right, dims)


def places():
    rows = lax.broadcasted_iota(jnp.int32, (CHUNK, CHUNK), 0)
    columns = lax.broadcasted_iota(jnp.int32, (CHUNK, CHUNK), 1)
    return rows, columns


def segments(doc_ref, c):
    rows, columns = places()
    row = doc_ref[c : c + 1, :].astype(F32)
    column = jnp.sum(jnp.where(rows == columns, row, 0.0), axis=1, keepdims=True)
    return row, column, row[:, :1], row[:, CHUNK - 1 :]


def chunk(c):
    return slice(c * CHUNK, (c + 1) * CHUNK)


def head(h):
    return slice(h * HEAD, (h + 1) * HEAD)


def as_number(flag):
    return flag.astype(F32)


def gates(lat_ref, w_ref, bias_ref):
    gate_pre = dot(lat_ref[...], w_ref[...], TN) + bias_ref[...]
    small = jnp.exp(-jnp.abs(gate_pre))
    series = small * (1.0 - small * (0.5 - small * (1.0 / 3.0 - small * (0.25 - small * 0.2))))
    log_one = jnp.where(small < 0.02, series, jnp.log(1.0 + small))
    log_gate = -(jnp.maximum(-gate_pre, 0.0) + log_one) / 16.0
    sigmoid = jnp.where(gate_pre >= 0.0, small, 1.0) / (1.0 + small)
    free = jnp.where(log_gate > -0.5, 1.0, jnp.where(log_gate == -0.5, 0.5, 0.0))
    return jnp.maximum(log_gate, -0.5), free * sigmoid * (1.0 / 16.0)


def decays(log_gate):
    rows, columns = places()
    lower3 = jnp.concatenate([(rows >= columns).astype(BF16)] * 3, axis=1)
    return [
        dot(lower3, jnp.concatenate(split3(log_gate[chunk(c), :]), axis=0), NN) for c in range(PARTS)
    ]


def state_kernel(ins, outs, need, emit):
    lat_ref, w_ref, bias_ref, doc_ref, k_ref, v_ref, q_ref, d_ref = ins
    send_ref, gate_ref, state_ref = outs
    heads = q_ref.shape[1] // HEAD
    need(0, 1, 2, 3)
    log_gate, gate_ref[1] = gates(lat_ref, w_ref, bias_ref)
    decay = decays(log_gate)
    for c in range(PARTS):
        gate_ref[0, chunk(c), :] = decay[c]
    emit(1, slice(None))
    seg = [segments(doc_ref, c) for c in range(PARTS)]
    first, last = seg[0][2], seg[-1][3]
    ends = [decay[c][CHUNK - 1 :, :] for c in range(PARTS)]
    grow = [jnp.exp(decay[c]) * (as_number(seg[c][1] == seg[c][2]) * SCALE) for c in range(PARTS)]
    rest = [jnp.exp(ends[c] - decay[c]) * as_number(seg[c][1] == seg[c][3]) for c in range(PARTS)]
    keep = [jnp.exp(ends[c]) * as_number(seg[c][2] == seg[c][3]) for c in range(PARTS)]
    link = [as_number(seg[c][2] == seg[c - 1][3]) for c in range(1, PARTS)]
    whole = jnp.exp(sum(ends)) * as_number(first == last)
    need(4, 5, 6, 7)
    each = HEAD // RING
    for h in range(heads):
        on = head(h)
        for c in range(PARTS):
            at = chunk(c)
            added = dot_left(v_ref[at, on], split2(k_ref[at, on].astype(F32) * rest[c][:, on]), TN)
            state_ref[0, h, c] = added
            state_ref[1, h, c] = dot_left(
                d_ref[at, on], split2(q_ref[at, on].astype(F32) * grow[c][:, on]), TN
            )
            memory = added if c == 0 else added + keep[c][:, on] * link[c - 1] * memory
        emit(2, (slice(None), h))
        back = state_ref[1, h, PARTS - 1]
        for c in reversed(range(PARTS - 1)):
            back = state_ref[1, h, c] + keep[c][:, on] * link[c] * back
        for j in range(RING):
            send_ref[j, h * each : (h + 1) * each, :] = memory[j * each : (j + 1) * each, :]
            start = heads * each + h * each
            send_ref[j, start : start + each, :] = back[j * each : (j + 1) * each, :]
    small_rows = jnp.concatenate(
        [whole[:, head(h)] for h in range(heads)]
        + [jnp.broadcast_to(first + 1.0, (1, HEAD)), jnp.broadcast_to(last + 1.0, (1, HEAD))]
        + [jnp.zeros((4, HEAD), F32)],
        axis=0,
    )
    for j in range(RING):
        send_ref[j, 64:, :] = small_rows
    emit(0, slice(None))


def taken(got_ref, j):
    factor = jnp.concatenate(
        [jnp.broadcast_to(got_ref[j, 64 + h : 65 + h, :], (16, HEAD)) for h in range(2)], axis=0
    )
    return got_ref[j, 0:32, :], got_ref[j, 32:64, :], factor, got_ref[j, 66:67, :], got_ref[j, 67:68, :]


def total_kernel(got_ref, sum_ref, ahead_ref, behind_ref):
    got = [taken(got_ref, j) for j in range(RING)]
    memory = got[0][0]
    for j in range(1, RING):
        memory = got[j][0] + got[j][2] * as_number(got[j][3] == got[j - 1][4]) * memory
    back = got[-1][1]
    for j in reversed(range(RING - 1)):
        back = got[j][1] + got[j][2] * as_number(got[j][4] == got[j + 1][3]) * back
    zeros = jnp.zeros((7, HEAD), F32)
    ahead_ref[...] = jnp.concatenate([memory, got[-1][4], zeros], axis=0)
    behind_ref[...] = jnp.concatenate([back, got[0][3], zeros], axis=0)


def spread_kernel(got_ref, ahead_ref, behind_ref, send_ref):
    got = [taken(got_ref, j) for j in range(RING)]
    memory = as_number(got[0][3] == ahead_ref[32:33, :]) * ahead_ref[0:32, :]
    for j in range(RING):
        send_ref[j, 0:32, :] = memory
        if j < RING - 1:
            memory = as_number(got[j][4] == got[j + 1][3]) * (got[j][0] + got[j][2] * memory)
    back = as_number(got[-1][4] == behind_ref[32:33, :]) * behind_ref[0:32, :]
    for j in reversed(range(RING)):
        send_ref[j, 32:64, :] = back
        if j > 0:
            back = as_number(got[j - 1][4] == got[j][3]) * (got[j][1] + got[j][2] * back)


def backward_sums(change, mask):
    return dot_left(mask, split3(change), NN)


def gate_sums(grad_pre, lat_ref, w_ref):
    heads = len(grad_pre[0])
    parts = [[split2(x) for x in row] for row in grad_pre]
    w = w_ref[...]
    lat_parts = []
    for c in range(PARTS):
        pre = [jnp.concatenate([parts[c][h][i] for h in range(heads)], axis=1) for i in range(2)]
        lat_parts.append(dot(w, pre[0], NT) + dot(w, pre[1], NT))
    lat = jnp.concatenate([lat_ref[...]] * 2, axis=1)
    grad_w, grad_b = [], []
    for h in range(heads):
        column = [parts[c][h][i] for i in range(2) for c in range(PARTS)]
        grad_w.append(dot(lat, jnp.concatenate(column, axis=0), NN))
        total = sum(grad_pre[c][h] for c in range(PARTS))
        grad_b.append(jnp.sum(total, axis=0, keepdims=True))
    zeros = jnp.zeros((6, HEAD), F32)
    return jnp.concatenate(lat_parts, axis=0), jnp.concatenate(grad_w + grad_b + [zeros], axis=0)


def inner_kernel(ins, outs, need, emit):
    lat_ref, w_ref, bias_ref, doc_ref, k_ref, v_ref, q_ref, d_ref = ins
    term_ref, sum_ref = outs
    heads = q_ref.shape[1] // HEAD
    rows, columns = places()
    log_gate, slope = gates(lat_ref, w_ref, bias_ref)
    decays_here = decays(log_gate)
    grad_pre = [[None] * heads for _ in range(PARTS)]
    for c in range(PARTS):
        row, column, _, _ = segments(doc_ref, c)
        same = column == row
        mask = (rows >= columns) & same
        later = ((columns >= rows) & same).astype(BF16)
        at = chunk(c)
        for h in range(heads):
            on = head(h)
            v, d = v_ref[at, on], d_ref[at, on]
            q32, k32 = q_ref[at, on].astype(F32), k_ref[at, on].astype(F32)
            decay = decays_here[c][:, on]
            grow, shrink = jnp.exp(decay), jnp.exp(-decay)
            qd, kd = split2(q32 * grow), split2(k32 * shrink)
            scores = split2(jnp.where(mask, dot_both(qd, kd, NT), 0.0))
            pulls = split2(jnp.where(mask, dot(d, v, NT), 0.0))
            term_ref[0, at, on] = dot_right(scores, v, NN) * SCALE
            term_ref[3, at, on] = dot_right(scores, d, TN) * SCALE
            dq = dot_both(pulls, kd, NN) * (grow * SCALE)
            dk = dot_both(pulls, qd, TN) * (shrink * SCALE)
            term_ref[1, at, on] = dq
            term_ref[2, at, on] = dk
            grad_pre[c][h] = backward_sums(q32 * dq - k32 * dk, later) * slope[at, on]
        emit(0, (slice(None), at))
    sum_ref[: PARTS * RANK, :], sum_ref[PARTS * RANK :, :] = gate_sums(grad_pre, lat_ref, w_ref)


def carry(h, seg, gate_ref, state_ref, got_ref):
    memory = got_ref[:, h * 16 : (h + 1) * 16, :].reshape(HEAD, HEAD)
    back = got_ref[:, 32 + h * 16 : 48 + h * 16, :].reshape(HEAD, HEAD)
    starts, ends, backs, keeps = [], [], [None] * PARTS, []
    for c in range(PARTS):
        _, _, first, last = seg[c]
        end = gate_ref[0, (c + 1) * CHUNK - 1 : (c + 1) * CHUNK, head(h)]
        keeps.append(jnp.exp(end) * as_number(first == last))
        if c > 0:
            memory = memory * as_number(first == seg[c - 1][3])
        starts.append(memory)
        memory = state_ref[0, h, c] + keeps[c] * memory
        ends.append(memory)
    for c in reversed(range(PARTS)):
        backs[c] = back
        if c > 0:
            back = as_number(seg[c][2] == seg[c - 1][3]) * (state_ref[1, h, c] + keeps[c] * back)
    return starts, ends, backs


def crossing(seg, c, h, q_ref, k_ref, v_ref, d_ref, gate_ref, start, behind):
    at, on = chunk(c), head(h)
    _, column, first, last = seg[c]
    decay = gate_ref[0, at, on]
    grow = jnp.exp(decay) * as_number(column == first)
    rest = jnp.exp(decay[CHUNK - 1 :, :] - decay) * as_number(column == last)
    dq = dot_left(d_ref[at, on], start, NN) * (grow * SCALE)
    dk = dot_left(v_ref[at, on], behind, NN) * rest
    return q_ref[at, on].astype(F32), k_ref[at, on].astype(F32), grow, rest, dq, dk


def grad_kernel(ins, outs, need, emit):
    got_ref, doc_ref, gate_ref, state_ref, v_ref, d_ref, q_ref, k_ref, lat_ref, w_ref, sum_ref = ins
    lat_send_ref, w_send_ref = outs
    heads = q_ref.shape[1] // HEAD
    rows, columns = places()
    seg = [segments(doc_ref, c) for c in range(PARTS)]
    later = [((columns >= rows) & (seg[c][1] == seg[c][0])).astype(BF16) for c in range(PARTS)]
    carried = [carry(h, seg, gate_ref, state_ref, got_ref) for h in range(heads)]
    grad_pre = [[None] * heads for _ in range(PARTS)]
    for h in range(heads):
        starts, ends, backs = carried[h]
        for c in range(PARTS):
            q32, k32, _, _, dq, dk = crossing(
                seg, c, h, q_ref, k_ref, v_ref, d_ref, gate_ref, split2(starts[c]), split2(backs[c])
            )
            through = jnp.sum(ends[c] * backs[c], axis=0, keepdims=True)
            tail = as_number(seg[c][1] == seg[c][3])
            grad_gate = backward_sums(q32 * dq - k32 * dk, later[c]) + tail * through
            grad_pre[c][h] = grad_gate * gate_ref[1, chunk(c), head(h)]
    lat_sum, w_sum = gate_sums(grad_pre, lat_ref, w_ref)
    lat_send_ref[...] = lat_sum + sum_ref[: PARTS * RANK, :]
    w_sum = w_sum + sum_ref[PARTS * RANK :, :]
    for j in range(RING):
        w_send_ref[j] = w_sum


def outer_kernel(ins, outs, need, emit):
    got_ref, doc_ref, gate_ref, state_ref, v_ref, d_ref, q_ref, k_ref, term_ref = ins
    out_ref, dq_ref, dk_ref, dv_ref = outs
    heads = q_ref.shape[1] // HEAD
    need(0, 1, 2, 3)
    seg = [segments(doc_ref, c) for c in range(PARTS)]
    carried = [carry(h, seg, gate_ref, state_ref, got_ref) for h in range(heads)]
    need(4, 5, 6, 7, 8)
    for c in range(PARTS):
        at = chunk(c)
        for h in range(heads):
            on = head(h)
            start, behind = split2(carried[h][0][c]), split2(carried[h][2][c])
            q32, k32, grow, rest, dq, dk = crossing(
                seg, c, h, q_ref, k_ref, v_ref, d_ref, gate_ref, start, behind
            )
            out = dot_both(split2(q32 * grow), start, NT) * SCALE
            dv = dot_both(split2(k32 * rest), behind, NT)
            out_ref[at, on] = (term_ref[0, at, on] + out).astype(BF16)
            dq_ref[at, on] = (term_ref[1, at, on] + dq).astype(BF16)
            dk_ref[at, on] = (term_ref[2, at, on] + dk).astype(BF16)
            dv_ref[at, on] = (term_ref[3, at, on] + dv).astype(BF16)
        for i in range(4):
            emit(i, at)


def resend_kernel(got_ref, lat_ref, lat_got_ref, send_ref, lat_send_ref):
    total = got_ref[0]
    for j in range(1, RING):
        total = total + got_ref[j]
    for j in range(RING):
        send_ref[j] = total
    lat_send_ref[...] = lat_ref[...] + lat_got_ref[...]


def finish_kernel(lat_mine_ref, lat_got_ref, w_got_ref, lat_ref, w_ref, b_ref):
    total = lat_mine_ref[...] + lat_got_ref[...]
    for c in range(PARTS):
        lat_ref[:, c * CHUNK : (c + 1) * CHUNK] = total[c * RANK : (c + 1) * RANK, :]
    total = w_got_ref[0]
    for j in range(1, RING):
        total = total + w_got_ref[j]
    for h in range(2):
        on = slice(h * HEAD, (h + 1) * HEAD)
        w_ref[:, on] = total[h * RANK : (h + 1) * RANK, :]
        b_ref[:, on] = total[2 * RANK + h : 2 * RANK + h + 1, :]


def estimate(operands, flops):
    moved = sum(x.size * x.dtype.itemsize for x in operands)
    return pl.CostEstimate(flops=flops, bytes_accessed=moved, transcendentals=0)


def call(kernel, outs, *operands):
    return pl.pallas_call(
        kernel,
        out_shape=outs,
        in_specs=[pl.BlockSpec(memory_space=pltpu.VMEM)] * len(operands),
        out_specs=jax.tree.map(lambda _: pl.BlockSpec(memory_space=pltpu.VMEM), outs),
        cost_estimate=estimate(operands, 10**10),
        compiler_params=pltpu.CompilerParams(vmem_limit_bytes=16 * 2**20),
    )(*operands)


def call_streamed(kernel, outs, *operands, flops, read=True, write=None, limit=60):
    n, m = len(operands), len(outs)
    pieces = 16
    write = tuple(range(m)) if write is None else write

    def run(*refs):
        sources, results, refs = refs[:n], refs[n : n + m], refs[n + m :]
        ins, refs = (refs[:n], refs[n:]) if read else (sources, refs)
        held = list(results)
        for i, buffer in zip(write, refs, strict=False):
            held[i] = buffer
        arrived, sent = refs[-2:]
        copies = [pltpu.make_async_copy(sources[i], ins[i], arrived.at[i]) for i in range(n)] if read else []
        for copy in copies:
            copy.start()
        going = []

        def need(*which):
            for i in which if read else ():
                copies[i].wait()

        def emit(i, at):
            if i in write:
                copy = pltpu.make_async_copy(held[i].at[at], results[i].at[at], sent.at[len(going)])
                copy.start()
                going.append(copy)

        kernel(ins, held, need, emit)
        for copy in going:
            copy.wait()

    spaces = (pltpu.VMEM, pltpu.HBM)
    buffers = [pltpu.VMEM(x.shape, x.dtype) for x in (operands if read else ())]
    buffers += [pltpu.VMEM(outs[i].shape, outs[i].dtype) for i in write]
    return pl.pallas_call(
        run,
        out_shape=outs,
        in_specs=[pl.BlockSpec(memory_space=spaces[read])] * n,
        out_specs=tuple(pl.BlockSpec(memory_space=spaces[i in write]) for i in range(m)),
        scratch_shapes=[*buffers, pltpu.SemaphoreType.DMA((n,)), pltpu.SemaphoreType.DMA((pieces,))],
        cost_estimate=estimate(operands, flops),
        compiler_params=pltpu.CompilerParams(vmem_limit_bytes=limit * 2**20),
    )(*operands)


def shape(dims, kind=F32):
    return jax.ShapeDtypeStruct(dims, kind)


def exchange(x, axis):
    return lax.all_to_all(x, axis, 0, 0)


def passed(value, axis, steps):
    count = lax.axis_size(axis)
    pairs = [(s, s + steps) for s in range(count) if 0 <= s + steps < count]
    return lax.ppermute(value, axis, pairs)


def swapped(value, axis, bit):
    return lax.ppermute(value, axis, [(s, s ^ bit) for s in range(lax.axis_size(axis))])


def body(query, key_in, value, latent, w_b, gate_bias, doc_ids, d_out):
    tokens, width = query.shape
    heads = width // HEAD
    lat = latent.T
    docs = doc_ids.reshape(PARTS, CHUNK)
    half = shape((tokens, width), BF16)
    ring = shape((RING, 40, HEAD))
    lat_shape = shape((PARTS * RANK, HEAD))
    gate_shape, state_shape = shape((2, tokens, width)), shape((2, heads, PARTS, HEAD, HEAD))
    rows = (value, d_out, query, key_in)
    operands = (lat, w_b, gate_bias.reshape(1, width), docs, key_in, value, query, d_out)
    send, gate, state = call_streamed(
        state_kernel, (shape((RING, 72, HEAD)), gate_shape, state_shape),
        *operands, flops=10**9,
    )
    terms, sums = call_streamed(
        inner_kernel, (shape((4, tokens, width)), shape((PARTS * RANK + 40, HEAD))),
        *operands, flops=INNER_FLOPS, read=False, write=(0,), limit=INNER_HELD,
    )
    got = exchange(send, "y")
    ahead, behind = call(total_kernel, (shape((40, HEAD)), shape((40, HEAD))), got, sums)
    ahead, behind = passed(ahead, "z", 1), passed(behind, "z", -1)
    carried = exchange(call(spread_kernel, shape((RING, 64, HEAD)), got, ahead, behind), "y")
    common = (carried, docs, gate, state, *rows)
    lat_send, w_send = call_streamed(
        grad_kernel, (lat_shape, ring), *common, lat, w_b, sums,
        flops=2 * 10**9, read=False, write=(), limit=HELD,
    )
    results = call_streamed(
        outer_kernel, (half, half, half, half), *common, terms, flops=3 * 10**9
    )
    w_got = exchange(w_send, "y")
    lat_send = jnp.sum(lax.all_gather(lat_send, "core"), axis=0)
    w_send, lat_send = call(
        resend_kernel, (ring, lat_shape), w_got, lat_send, swapped(lat_send, "x", 2)
    )
    w_got = exchange(w_send, "z")
    lat_got = swapped(lat_send, "x", 1)
    grad_lat, grad_w, grad_b = call(
        finish_kernel, (shape((RANK, tokens)), shape((RANK, width)), shape((1, width))),
        lat_send, lat_got, w_got,
    )
    return *results, grad_lat.T, grad_w, grad_b.reshape(width)


def solution(mesh):
    grid = Mesh(mesh.devices.reshape(4, 2, RING, RING), ("x", "core", "z", "y"))
    rows = P(CTX, DP)
    in_specs = (rows, rows, rows, P(CTX, None), P(None, DP), P(DP), P(CTX), rows)
    out_specs = (rows, rows, rows, rows, P(CTX, None), P(None, DP), P(DP))
    return jax.shard_map(body, mesh=grid, in_specs=in_specs, out_specs=out_specs, check_vma=False)
```

```python
import jax
import jax.numpy as jnp
from jax import lax
from jax.experimental import pallas as pl
from jax.experimental.pallas import tpu as pltpu
from jax.sharding import Mesh
from jax.sharding import PartitionSpec as P

HEAD = 128
RANK = 16
SPAN = 512
CHUNK = 128
PARTS = SPAN // CHUNK
SCALE = HEAD ** (-0.5)
RING = 8
HELD = 16
INNER_HELD = 16
INNER_FLOPS = 4 * 10**10
CTX = ("z", "y")
DP = ("x", "core")

F32 = jnp.float32
BF16 = jnp.bfloat16
NN = (((1,), (0,)), ((), ()))
NT = (((1,), (1,)), ((), ()))
TN = (((0,), (0,)), ((), ()))


def split2(x):
    high = x.astype(BF16)
    return high, (x - high.astype(F32)).astype(BF16)


def split3(x):
    high = x.astype(BF16)
    rest = x - high.astype(F32)
    middle = rest.astype(BF16)
    return high, middle, (rest - middle.astype(F32)).astype(BF16)


def dot(a, b, dims):
    return lax.dot_general(a, b, dims, preferred_element_type=F32)


def dot_left(a, parts, dims):
    (ca,), (cb,) = dims[0]
    return dot(jnp.concatenate([a] * len(parts), axis=ca), jnp.concatenate(parts, axis=cb), dims)


def dot_right(parts, b, dims):
    (ca,), (cb,) = dims[0]
    return dot(jnp.concatenate(parts, axis=ca), jnp.concatenate([b] * len(parts), axis=cb), dims)


def dot_both(a, b, dims):
    (ca,), (cb,) = dims[0]
    left = jnp.concatenate([a[0], a[1], a[0]], axis=ca)
    right = jnp.concatenate([b[0], b[0], b[1]], axis=cb)
    return dot(left, right, dims)


def places():
    rows = lax.broadcasted_iota(jnp.int32, (CHUNK, CHUNK), 0)
    columns = lax.broadcasted_iota(jnp.int32, (CHUNK, CHUNK), 1)
    return rows, columns


def segments(doc_ref, c):
    rows, columns = places()
    row = doc_ref[c : c + 1, :].astype(F32)
    column = jnp.sum(jnp.where(rows == columns, row, 0.0), axis=1, keepdims=True)
    return row, column, row[:, :1], row[:, CHUNK - 1 :]


def chunk(c):
    return slice(c * CHUNK, (c + 1) * CHUNK)


def head(h):
    return slice(h * HEAD, (h + 1) * HEAD)


def as_number(flag):
    return flag.astype(F32)


def gates(lat_ref, w_ref, bias_ref):
    gate_pre = dot(lat_ref[...], w_ref[...], TN) + bias_ref[...]
    small = jnp.exp(-jnp.abs(gate_pre))
    series = small * (1.0 - small * (0.5 - small * (1.0 / 3.0 - small * (0.25 - small * 0.2))))
    log_one = jnp.where(small < 0.02, series, jnp.log(1.0 + small))
    log_gate = -(jnp.maximum(-gate_pre, 0.0) + log_one) / 16.0
    sigmoid = jnp.where(gate_pre >= 0.0, small, 1.0) / (1.0 + small)
    free = jnp.where(log_gate > -0.5, 1.0, jnp.where(log_gate == -0.5, 0.5, 0.0))
    return jnp.maximum(log_gate, -0.5), free * sigmoid * (1.0 / 16.0)


def decays(log_gate):
    rows, columns = places()
    lower3 = jnp.concatenate([(rows >= columns).astype(BF16)] * 3, axis=1)
    return [
        dot(lower3, jnp.concatenate(split3(log_gate[chunk(c), :]), axis=0), NN) for c in range(PARTS)
    ]


def state_kernel(ins, outs, need, emit):
    lat_ref, w_ref, bias_ref, doc_ref, k_ref, v_ref, q_ref, d_ref = ins
    send_ref, gate_ref, state_ref = outs
    heads = q_ref.shape[1] // HEAD
    need(0, 1, 2, 3)
    log_gate, gate_ref[1] = gates(lat_ref, w_ref, bias_ref)
    decay = decays(log_gate)
    for c in range(PARTS):
        gate_ref[0, chunk(c), :] = decay[c]
    emit(1, slice(None))
    seg = [segments(doc_ref, c) for c in range(PARTS)]
    first, last = seg[0][2], seg[-1][3]
    ends = [decay[c][CHUNK - 1 :, :] for c in range(PARTS)]
    grow = [jnp.exp(decay[c]) * (as_number(seg[c][1] == seg[c][2]) * SCALE) for c in range(PARTS)]
    rest = [jnp.exp(ends[c] - decay[c]) * as_number(seg[c][1] == seg[c][3]) for c in range(PARTS)]
    keep = [jnp.exp(ends[c]) * as_number(seg[c][2] == seg[c][3]) for c in range(PARTS)]
    link = [as_number(seg[c][2] == seg[c - 1][3]) for c in range(1, PARTS)]
    whole = jnp.exp(sum(ends)) * as_number(first == last)
    need(4, 5, 6, 7)
    each = HEAD // RING
    for h in range(heads):
        on = head(h)
        for c in range(PARTS):
            at = chunk(c)
            added = dot_left(v_ref[at, on], split2(k_ref[at, on].astype(F32) * rest[c][:, on]), TN)
            state_ref[0, h, c] = added
            state_ref[1, h, c] = dot_left(
                d_ref[at, on], split2(q_ref[at, on].astype(F32) * grow[c][:, on]), TN
            )
            memory = added if c == 0 else added + keep[c][:, on] * link[c - 1] * memory
        emit(2, (slice(None), h))
        back = state_ref[1, h, PARTS - 1]
        for c in reversed(range(PARTS - 1)):
            back = state_ref[1, h, c] + keep[c][:, on] * link[c] * back
        for j in range(RING):
            send_ref[j, h * each : (h + 1) * each, :] = memory[j * each : (j + 1) * each, :]
            start = heads * each + h * each
            send_ref[j, start : start + each, :] = back[j * each : (j + 1) * each, :]
    small_rows = jnp.concatenate(
        [whole[:, head(h)] for h in range(heads)]
        + [jnp.broadcast_to(first + 1.0, (1, HEAD)), jnp.broadcast_to(last + 1.0, (1, HEAD))]
        + [jnp.zeros((4, HEAD), F32)],
        axis=0,
    )
    for j in range(RING):
        send_ref[j, 64:, :] = small_rows
    emit(0, slice(None))


def taken(got_ref, j):
    factor = jnp.concatenate(
        [jnp.broadcast_to(got_ref[j, 64 + h : 65 + h, :], (16, HEAD)) for h in range(2)], axis=0
    )
    return got_ref[j, 0:32, :], got_ref[j, 32:64, :], factor, got_ref[j, 66:67, :], got_ref[j, 67:68, :]


def total_kernel(got_ref, sum_ref, ahead_ref, behind_ref):
    got = [taken(got_ref, j) for j in range(RING)]
    memory = got[0][0]
    for j in range(1, RING):
        memory = got[j][0] + got[j][2] * as_number(got[j][3] == got[j - 1][4]) * memory
    back = got[-1][1]
    for j in reversed(range(RING - 1)):
        back = got[j][1] + got[j][2] * as_number(got[j][4] == got[j + 1][3]) * back
    zeros = jnp.zeros((7, HEAD), F32)
    ahead_ref[...] = jnp.concatenate([memory, got[-1][4], zeros], axis=0)
    behind_ref[...] = jnp.concatenate([back, got[0][3], zeros], axis=0)


def spread_kernel(got_ref, ahead_ref, behind_ref, send_ref):
    got = [taken(got_ref, j) for j in range(RING)]
    memory = as_number(got[0][3] == ahead_ref[32:33, :]) * ahead_ref[0:32, :]
    for j in range(RING):
        send_ref[j, 0:32, :] = memory
        if j < RING - 1:
            memory = as_number(got[j][4] == got[j + 1][3]) * (got[j][0] + got[j][2] * memory)
    back = as_number(got[-1][4] == behind_ref[32:33, :]) * behind_ref[0:32, :]
    for j in reversed(range(RING)):
        send_ref[j, 32:64, :] = back
        if j > 0:
            back = as_number(got[j - 1][4] == got[j][3]) * (got[j][1] + got[j][2] * back)


def backward_sums(change, mask):
    return dot_left(mask, split3(change), NN)


def gate_sums(grad_pre, lat_ref, w_ref):
    heads = len(grad_pre[0])
    parts = [[split2(x) for x in row] for row in grad_pre]
    w = w_ref[...]
    lat_parts = []
    for c in range(PARTS):
        pre = [jnp.concatenate([parts[c][h][i] for h in range(heads)], axis=1) for i in range(2)]
        lat_parts.append(dot(w, pre[0], NT) + dot(w, pre[1], NT))
    lat = jnp.concatenate([lat_ref[...]] * 2, axis=1)
    grad_w, grad_b = [], []
    for h in range(heads):
        column = [parts[c][h][i] for i in range(2) for c in range(PARTS)]
        grad_w.append(dot(lat, jnp.concatenate(column, axis=0), NN))
        total = sum(grad_pre[c][h] for c in range(PARTS))
        grad_b.append(jnp.sum(total, axis=0, keepdims=True))
    zeros = jnp.zeros((6, HEAD), F32)
    return jnp.concatenate(lat_parts, axis=0), jnp.concatenate(grad_w + grad_b + [zeros], axis=0)


def inner_kernel(ins, outs, need, emit):
    lat_ref, w_ref, bias_ref, doc_ref, k_ref, v_ref, q_ref, d_ref = ins
    term_ref, sum_ref = outs
    heads = q_ref.shape[1] // HEAD
    rows, columns = places()
    log_gate, slope = gates(lat_ref, w_ref, bias_ref)
    decays_here = decays(log_gate)
    grad_pre = [[None] * heads for _ in range(PARTS)]
    for c in range(PARTS):
        row, column, _, _ = segments(doc_ref, c)
        same = column == row
        mask = (rows >= columns) & same
        later = ((columns >= rows) & same).astype(BF16)
        at = chunk(c)
        for h in range(heads):
            on = head(h)
            v, d = v_ref[at, on], d_ref[at, on]
            q32, k32 = q_ref[at, on].astype(F32), k_ref[at, on].astype(F32)
            decay = decays_here[c][:, on]
            grow, shrink = jnp.exp(decay), jnp.exp(-decay)
            qd, kd = split2(q32 * grow), split2(k32 * shrink)
            scores = split2(jnp.where(mask, dot_both(qd, kd, NT), 0.0))
            pulls = split2(jnp.where(mask, dot(d, v, NT), 0.0))
            term_ref[0, at, on] = dot_right(scores, v, NN) * SCALE
            term_ref[3, at, on] = dot_right(scores, d, TN) * SCALE
            dq = dot_both(pulls, kd, NN) * (grow * SCALE)
            dk = dot_both(pulls, qd, TN) * (shrink * SCALE)
            term_ref[1, at, on] = dq
            term_ref[2, at, on] = dk
            grad_pre[c][h] = backward_sums(q32 * dq - k32 * dk, later) * slope[at, on]
        emit(0, (slice(None), at))
    sum_ref[: PARTS * RANK, :], sum_ref[PARTS * RANK :, :] = gate_sums(grad_pre, lat_ref, w_ref)


def carry(h, seg, gate_ref, state_ref, got_ref, whole=True):
    memory = got_ref[:, h * 16 : (h + 1) * 16, :].reshape(HEAD, HEAD)
    back = got_ref[:, 32 + h * 16 : 48 + h * 16, :].reshape(HEAD, HEAD)
    starts, ends, backs, keeps = [], [], [None] * PARTS, []
    for c in range(PARTS):
        _, _, first, last = seg[c]
        end = gate_ref[0, (c + 1) * CHUNK - 1 : (c + 1) * CHUNK, head(h)]
        keeps.append(jnp.exp(end) * as_number(first == last))
        if c > 0:
            memory = memory * as_number(first == seg[c - 1][3])
        starts.append(memory)
        if whole or c < PARTS - 1:
            memory = state_ref[0, h, c] + keeps[c] * memory
            ends.append(memory)
    for c in reversed(range(PARTS)):
        backs[c] = back
        if c > 0:
            back = as_number(seg[c][2] == seg[c - 1][3]) * (state_ref[1, h, c] + keeps[c] * back)
    return starts, ends, backs


def crossing(seg, c, h, q_ref, k_ref, v_ref, d_ref, gate_ref, start, behind):
    at, on = chunk(c), head(h)
    _, column, first, last = seg[c]
    decay = gate_ref[0, at, on]
    grow = jnp.exp(decay) * as_number(column == first)
    rest = jnp.exp(decay[CHUNK - 1 :, :] - decay) * as_number(column == last)
    dq = dot_left(d_ref[at, on], start, NN) * (grow * SCALE)
    dk = dot_left(v_ref[at, on], behind, NN) * rest
    return q_ref[at, on].astype(F32), k_ref[at, on].astype(F32), grow, rest, dq, dk


def grad_kernel(ins, outs, need, emit):
    got_ref, doc_ref, gate_ref, state_ref, v_ref, d_ref, q_ref, k_ref, lat_ref, w_ref, sum_ref = ins
    lat_send_ref, w_send_ref = outs
    heads = q_ref.shape[1] // HEAD
    rows, columns = places()
    seg = [segments(doc_ref, c) for c in range(PARTS)]
    later = [((columns >= rows) & (seg[c][1] == seg[c][0])).astype(BF16) for c in range(PARTS)]
    carried = [carry(h, seg, gate_ref, state_ref, got_ref) for h in range(heads)]
    grad_pre = [[None] * heads for _ in range(PARTS)]
    for h in range(heads):
        starts, ends, backs = carried[h]
        for c in range(PARTS):
            q32, k32, _, _, dq, dk = crossing(
                seg, c, h, q_ref, k_ref, v_ref, d_ref, gate_ref, split2(starts[c]), split2(backs[c])
            )
            through = jnp.sum(ends[c] * backs[c], axis=0, keepdims=True)
            tail = as_number(seg[c][1] == seg[c][3])
            grad_gate = backward_sums(q32 * dq - k32 * dk, later[c]) + tail * through
            grad_pre[c][h] = grad_gate * gate_ref[1, chunk(c), head(h)]
    lat_sum, w_sum = gate_sums(grad_pre, lat_ref, w_ref)
    lat_send_ref[...] = lat_sum + sum_ref[: PARTS * RANK, :]
    w_sum = w_sum + sum_ref[PARTS * RANK :, :]
    for j in range(RING):
        w_send_ref[j] = w_sum


def outer_kernel(ins, outs, need, emit):
    got_ref, doc_ref, gate_ref, state_ref, v_ref, d_ref, q_ref, k_ref, term_ref = ins
    out_ref, dq_ref, dk_ref, dv_ref = outs
    heads = q_ref.shape[1] // HEAD
    need(0, 1, 2, 3)
    seg = [segments(doc_ref, c) for c in range(PARTS)]
    carried = [carry(h, seg, gate_ref, state_ref, got_ref, False) for h in range(heads)]
    need(4, 5, 6, 7, 8)
    for c in range(PARTS):
        at = chunk(c)
        for h in range(heads):
            on = head(h)
            start, behind = split2(carried[h][0][c]), split2(carried[h][2][c])
            q32, k32, grow, rest, dq, dk = crossing(
                seg, c, h, q_ref, k_ref, v_ref, d_ref, gate_ref, start, behind
            )
            out = dot_both(split2(q32 * grow), start, NT) * SCALE
            dv = dot_both(split2(k32 * rest), behind, NT)
            out_ref[at, on] = (term_ref[0, at, on] + out).astype(BF16)
            dq_ref[at, on] = (term_ref[1, at, on] + dq).astype(BF16)
            dk_ref[at, on] = (term_ref[2, at, on] + dk).astype(BF16)
            dv_ref[at, on] = (term_ref[3, at, on] + dv).astype(BF16)
        for i in range(4):
            emit(i, at)


def resend_kernel(got_ref, lat_ref, lat_got_ref, send_ref, lat_send_ref):
    total = got_ref[0]
    for j in range(1, RING):
        total = total + got_ref[j]
    for j in range(RING):
        send_ref[j] = total
    lat_send_ref[...] = lat_ref[...] + lat_got_ref[...]


def finish_kernel(lat_mine_ref, lat_got_ref, w_got_ref, lat_ref, w_ref, b_ref):
    total = lat_mine_ref[...] + lat_got_ref[...]
    for c in range(PARTS):
        lat_ref[:, c * CHUNK : (c + 1) * CHUNK] = total[c * RANK : (c + 1) * RANK, :]
    total = w_got_ref[0]
    for j in range(1, RING):
        total = total + w_got_ref[j]
    for h in range(2):
        on = slice(h * HEAD, (h + 1) * HEAD)
        w_ref[:, on] = total[h * RANK : (h + 1) * RANK, :]
        b_ref[:, on] = total[2 * RANK + h : 2 * RANK + h + 1, :]


def estimate(operands, flops):
    moved = sum(x.size * x.dtype.itemsize for x in operands)
    return pl.CostEstimate(flops=flops, bytes_accessed=moved, transcendentals=0)


def call(kernel, outs, *operands, flops=10**10):
    return pl.pallas_call(
        kernel,
        out_shape=outs,
        in_specs=[pl.BlockSpec(memory_space=pltpu.VMEM)] * len(operands),
        out_specs=jax.tree.map(lambda _: pl.BlockSpec(memory_space=pltpu.VMEM), outs),
        cost_estimate=estimate(operands, flops),
        compiler_params=pltpu.CompilerParams(vmem_limit_bytes=16 * 2**20),
    )(*operands)


def call_streamed(kernel, outs, *operands, flops, read=True, write=None, limit=60, taken=None):
    n, m = len(operands), len(outs)
    pieces = 16
    write = tuple(range(m)) if write is None else write
    taken = [(taken or {}).get(i, [slice(None)]) for i in range(n)]
    first = [sum(map(len, taken[:i])) for i in range(n + 1)]

    def run(*refs):
        sources, results, refs = refs[:n], refs[n : n + m], refs[n + m :]
        ins, refs = (refs[:n], refs[n:]) if read else (sources, refs)
        held = list(results)
        for i, buffer in zip(write, refs, strict=False):
            held[i] = buffer
        arrived, sent = refs[-2:]
        copies = [
            [
                pltpu.make_async_copy(sources[i].at[at], ins[i].at[at], arrived.at[first[i] + j])
                for j, at in enumerate(taken[i])
            ]
            for i in (range(n) if read else ())
        ]
        for group in copies:
            for copy in group:
                copy.start()
        going = []

        def need(*which):
            for i in which if read else ():
                for copy in copies[i]:
                    copy.wait()

        def emit(i, at):
            if i in write:
                copy = pltpu.make_async_copy(held[i].at[at], results[i].at[at], sent.at[len(going)])
                copy.start()
                going.append(copy)

        kernel(ins, held, need, emit)
        for copy in going:
            copy.wait()

    spaces = (pltpu.VMEM, pltpu.HBM)
    buffers = [pltpu.VMEM(x.shape, x.dtype) for x in (operands if read else ())]
    buffers += [pltpu.VMEM(outs[i].shape, outs[i].dtype) for i in write]
    return pl.pallas_call(
        run,
        out_shape=outs,
        in_specs=[pl.BlockSpec(memory_space=spaces[read])] * n,
        out_specs=tuple(pl.BlockSpec(memory_space=spaces[i in write]) for i in range(m)),
        scratch_shapes=[*buffers, pltpu.SemaphoreType.DMA((first[n],)), pltpu.SemaphoreType.DMA((pieces,))],
        cost_estimate=estimate(operands, flops),
        compiler_params=pltpu.CompilerParams(vmem_limit_bytes=limit * 2**20),
    )(*operands)


def shape(dims, kind=F32):
    return jax.ShapeDtypeStruct(dims, kind)


def exchange(x, axis):
    return lax.all_to_all(x, axis, 0, 0)


def passed(value, axis, steps):
    count = lax.axis_size(axis)
    pairs = [(s, s + steps) for s in range(count) if 0 <= s + steps < count]
    return lax.ppermute(value, axis, pairs)


def swapped(value, axis, bit):
    return lax.ppermute(value, axis, [(s, s ^ bit) for s in range(lax.axis_size(axis))])


def body(query, key_in, value, latent, w_b, gate_bias, doc_ids, d_out):
    tokens, width = query.shape
    heads = width // HEAD
    lat = latent.T
    docs = doc_ids.reshape(PARTS, CHUNK)
    half = shape((tokens, width), BF16)
    ring = shape((RING, 40, HEAD))
    lat_shape = shape((PARTS * RANK, HEAD))
    gate_shape, state_shape = shape((2, tokens, width)), shape((2, heads, PARTS, HEAD, HEAD))
    rows = (value, d_out, query, key_in)
    operands = (lat, w_b, gate_bias.reshape(1, width), docs, key_in, value, query, d_out)
    send, gate, state = call_streamed(
        state_kernel, (shape((RING, 72, HEAD)), gate_shape, state_shape),
        *operands, flops=10**9,
    )
    terms, sums = call_streamed(
        inner_kernel, (shape((4, tokens, width)), shape((PARTS * RANK + 40, HEAD))),
        *operands, flops=INNER_FLOPS, read=False, write=(), limit=INNER_HELD,
    )
    got = exchange(send, "y")
    ahead, behind = call(total_kernel, (shape((40, HEAD)), shape((40, HEAD))), got, sums)
    ahead, behind = passed(ahead, "z", 1), passed(behind, "z", -1)
    carried = exchange(call(spread_kernel, shape((RING, 64, HEAD)), got, ahead, behind), "y")
    common = (carried, docs, gate, state, *rows)
    lat_send, w_send = call_streamed(
        grad_kernel, (lat_shape, ring), *common, lat, w_b, sums,
        flops=2 * 10**9, read=False, write=(), limit=HELD,
    )
    results = call_streamed(
        outer_kernel, (half, half, half, half), *common, terms,
        flops=3 * 10**9, taken={2: [0], 3: [(0, slice(None), slice(0, 3)), (1, slice(None), slice(1, 4))]},
    )
    w_got = exchange(w_send, "y")
    lat_send = jnp.sum(lax.all_gather(lat_send, "core"), axis=0)
    w_send, lat_send = call(
        resend_kernel, (ring, lat_shape), w_got, lat_send, swapped(lat_send, "x", 1),
        flops=10**11,
    )
    w_got = exchange(w_send, "z")
    lat_got = swapped(lat_send, "x", 2)
    grad_lat, grad_w, grad_b = call(
        finish_kernel, (shape((RANK, tokens)), shape((RANK, width)), shape((1, width))),
        lat_send, lat_got, w_got,
    )
    return *results, grad_lat.T, grad_w, grad_b.reshape(width)


def solution(mesh):
    grid = Mesh(mesh.devices.reshape(4, 2, RING, RING), ("x", "core", "z", "y"))
    rows = P(CTX, DP)
    in_specs = (rows, rows, rows, P(CTX, None), P(None, DP), P(DP), P(CTX), rows)
    out_specs = (rows, rows, rows, rows, P(CTX, None), P(None, DP), P(DP))
    return jax.shard_map(body, mesh=grid, in_specs=in_specs, out_specs=out_specs, check_vma=False)
```
